512 devices in a mesh: expert: 64 (over z_hi, y, x), tensor: 8 (over z_lo, core).
Axes of the slice: x: 4, y: 4, z: 16 (z_hi: 4, z_lo: 4; z = z_hi * 4 + z_lo), core: 2. Of those that a mesh axis runs over, the one named last changes fastest.
Arguments:
- grad_out: bfloat16 [32768, 3072], P('expert', 'tensor'), may hold values from -6 to 6
- hidden_in: bfloat16 [32768, 4096], P('expert', 'tensor')
- gate_prob: float32 [32768], P('expert'), may hold values from 0.1 to 1
- expert_ids: int32 [32768, 1], P('expert'), may hold values from 0 to 63; in each aligned block of 512 rows (0 to 511, 512 to 1023, ...) at most 16 rows name the same one
- w_down: bfloat16 [64, 4096, 3072], P('expert', 'tensor'), may hold values from -0.09375 to 0.09375
Outputs:
- grad_hidden: bfloat16 [32768, 4096], P('expert', 'tensor')
- grad_gate: float32 [32768], P('expert')
The draws below stay inside these ranges and needn't reach their ends.
Inputs may be any that keep to these rules, and one draw needn't show every extreme that they name: `expert_ids`: in each aligned block of 512 tokens no expert is named more than 16 times, a bound that some block reaches.
All inputs are finite; a program needn't handle non-finite values.
Results may differ from the reference program's by a relative error of at most 0.0049.
Values may be sent and summed in bfloat16 or wider, within the bound.
No kernel may reach another device: no remote copies, remote signals or barrier semaphores. Data moves between devices by JAX's collectives and lax.ppermute only.
A program may use at most 64 MiB of HBM per device.

```python
import math
import jax
import jax.numpy as jnp
import numpy as np
from jax import lax

D = 3072
FF = 4096
TOK_DEV = 512
EXPERTS = 64
TOKENS = 32768
CAP = 16
N_EXPERT = 64


def draw_hidden_in(key, part):
    key = jax.random.fold_in(key, 7)
    first = jax.random.fold_in(key, 0)
    columns = jnp.arange(FF, dtype=jnp.float32)
    rising = jnp.exp(jnp.log(3.0) * columns / FF)[None, :]
    scale_all = 2.0 / jnp.sqrt(jnp.float32(FF))
    base = jax.random.normal(first, (TOKENS, FF), jnp.float32)
    values = base * rising * scale_all
    return values.astype(jnp.bfloat16)


def steps_of(key, dims, cuts, low, top_value):
    factor_of, own = 1.0, jax.random.fold_in(key, 6)
    for dim, shards_of in cuts:
        heights = jnp.exp(jax.random.uniform(jax.random.fold_in(own, dim), (shards_of,), jnp.float32, low / len(cuts), top_value / len(cuts)))
        factor_of = factor_of * jnp.repeat(heights, dims[dim] // shards_of).reshape([-1 if axis == dim else 1 for axis in range(len(dims))])
    return factor_of


def assign_block(rng, own, number, rows, count, top, most, skew):
    sequence = jax.random.permutation(rng, count)
    heavy_load, ordinary = portions_of(count, rows * top, most, skew, True), portions_of(count, rows * top, most, skew, False)
    places = jnp.arange(count)

    def named(tallies, offset_by):
        used = int((tallies > 0).sum())
        fixed = max(1, used // 4)
        moved = fixed + (places - fixed + offset_by * (used - fixed)) % max(1, count - fixed)
        return jnp.zeros((count,), jnp.int32).at[sequence[jnp.where(places < fixed, places, moved)]].set(jnp.asarray(tallies, jnp.int32))

    tallies = jnp.where(number % 4 == 0, named(heavy_load, number // 4), named(ordinary, number - number // 4 - 1))
    mixed = jax.random.permutation(jax.random.fold_in(own, 3), count)
    donor, sink = mixed[0:count // 2 * 2:2], mixed[1:count // 2 * 2:2]
    slack = jnp.minimum(tallies[donor] - 1, most - tallies[sink]) // 2
    slack = jnp.where((donor == sequence[0]) | (sink == sequence[0]) | (tallies[sink] == 0), 0, jnp.maximum(slack, 0))
    moved = jax.random.randint(jax.random.fold_in(own, 4), (count // 2,), 0, 1 << 20) % (slack + 1)
    tallies = tallies.at[donor].add(-moved).at[sink].add(moved)
    labels = jnp.searchsorted(jnp.cumsum(tallies), jnp.arange(rows * top), side="right").astype(jnp.int32)
    table = labels.reshape(top, rows).T
    table = table[jax.random.permutation(jax.random.fold_in(own, 1), rows)]
    offset_by = jax.random.randint(jax.random.fold_in(own, 2), (rows, 1), 0, top)
    return jnp.take_along_axis(table, (jnp.arange(top)[None, :] + offset_by) % top, axis=1)


def portions_of(count, total, bound, slope, full):
    portions = [(1 << 20) // math.isqrt(grade ** slope) + 1 for grade in range(1, count + 1)]
    largest = bound if full else min(bound, max(-(-total // count), total * portions[0] // sum(portions)))
    least = 1 if total - largest >= count - 1 else 0
    counts, rest = [largest] + [least] * (count - 1), total - largest - least * (count - 1)
    while rest > 0:
        candidates = [i for i in range(1, count) if counts[i] < largest] or [i for i in range(1, count) if counts[i] < bound]
        mass, left = sum([portions[i] for i in candidates]), rest
        for i in candidates:
            extra = min(bound - counts[i], max(1, left * portions[i] // mass), rest)
            counts[i] = counts[i] + extra
            rest = rest - extra
    return np.array(counts)


def centred(own_key, shape, spread, bound, shards=(), kind=jnp.bfloat16):
    factor_of = steps_of(own_key, shape, shards, -0.22, 0.18) if shards else 1.0
    entries = jax.random.normal(own_key, shape, jnp.float32) * spread * factor_of
    return jnp.minimum(jnp.maximum(entries, -bound), bound).astype(kind)


def setup_inputs(seed: int = 0) -> dict:
    streams_of = jax.random.split(jax.random.key(seed), 6)
    grad_out = centred(streams_of[0], (TOKENS, D), 1.0, 6.0, ((0, 64), (1, 8)))
    hidden_in = draw_hidden_in(jax.random.fold_in(streams_of[5], 71), 0)
    gate_prob = jnp.clip(jnp.exp(math.log(1.0) - 2.3025851 * jax.random.uniform(streams_of[2], (TOKENS,), jnp.float32) ** steps_of(streams_of[2], (TOKENS,), ((0, 64),), -0.2, 0.2)), 0.1, 1.0)
    expert_ids_keys = jax.random.split(jax.random.fold_in(streams_of[3], 1), TOKENS // TOK_DEV)
    expert_ids_turns = jax.random.permutation(jax.random.fold_in(streams_of[3], 3), TOKENS // TOK_DEV)
    expert_ids = jax.vmap(lambda own, number: assign_block(jax.random.fold_in(streams_of[3], 2), own, number, TOK_DEV, EXPERTS, 1, CAP, 2))(expert_ids_keys, expert_ids_turns).reshape((TOKENS, 1))
    w_down = centred(streams_of[4], (EXPERTS, FF, D), FF ** -0.5, 0.09375, ((0, 64), (1, 8)))
    return {"grad_out": grad_out, "hidden_in": hidden_in, "gate_prob": gate_prob, "expert_ids": expert_ids, "w_down": w_down}


def reference(grad_out, hidden_in, gate_prob, expert_ids, w_down):
    tokens = grad_out.shape[0]
    chosen = expert_ids[:, 0].astype(jnp.int32)
    onehot = (chosen[:, None] == jnp.arange(EXPERTS, dtype=jnp.int32)[None, :]).astype(jnp.int32)
    blocks = onehot.reshape(N_EXPERT, TOK_DEV, EXPERTS)
    earlier = jnp.sum((jnp.cumsum(blocks, axis=1) - 1) * blocks, axis=2).reshape(tokens).astype(jnp.int32)
    anchor = (jnp.arange(tokens, dtype=jnp.int32) // TOK_DEV).astype(jnp.int32)
    column = (anchor * CAP + earlier).astype(jnp.int32)
    table = jnp.full((EXPERTS, N_EXPERT * CAP), tokens, jnp.int32).at[chosen, column].set(jnp.arange(tokens, dtype=jnp.int32))
    padded = jnp.concatenate([grad_out, jnp.zeros((1, D), grad_out.dtype)], axis=0)

    def one_expert(pair):
        index, weight = pair
        return jnp.dot(padded[index], weight.T, preferred_element_type=jnp.float32).astype(jnp.bfloat16)

    rows = lax.map(one_expert, (table, w_down))
    returned = jnp.zeros((tokens + 1, FF), jnp.bfloat16).at[table.reshape(-1)].set(rows.reshape(-1, FF))
    returned = returned[:tokens].astype(jnp.float32)
    grad_hidden = (gate_prob[:, None] * returned).astype(jnp.bfloat16)
    grad_gate = jnp.sum(hidden_in.astype(jnp.float32) * returned, axis=1)
    return grad_hidden, grad_gate
```

```python
import jax
import jax.numpy as jnp
from jax import lax
from jax.sharding import PartitionSpec as P

CORES = 2


def line_pairs(chips, pairs):
    return [(a * CORES + c, b * CORES + c) for a, b in pairs for c in range(CORES)]


def body(grad_out, hidden_in, gate_prob, expert_ids, w_down):
    tokens, width = grad_out.shape
    groups = lax.axis_size("expert")
    shards = lax.axis_size("tensor")
    chips = shards // CORES
    local = w_down.shape[0]
    experts = local * groups
    capacity = 2 * tokens // experts
    slots = experts * capacity
    weight = w_down[0]
    bf16, f32 = jnp.bfloat16, jnp.float32

    with jax.named_scope("route"):
        chosen = expert_ids[:, 0]
        onehot = (chosen[:, None] == jnp.arange(experts, dtype=jnp.int32)[None, :]).astype(bf16)
        row = jnp.arange(tokens, dtype=jnp.int32)
        before = (row[None, :] < row[:, None]).astype(bf16)
        counts = jnp.dot(before, onehot, preferred_element_type=f32)
        earlier = jnp.sum(counts * onehot.astype(f32), axis=1).astype(jnp.int32)
        target = chosen * capacity + earlier
        place = (jnp.arange(slots, dtype=jnp.int32)[:, None] == target[None, :]).astype(bf16)
        send = jnp.dot(place, grad_out, preferred_element_type=f32).astype(bf16)

    with jax.named_scope("dispatch"):
        own = lax.all_to_all(send, "expert", split_axis=0, concat_axis=0, tiled=True)

    position = lax.axis_index("tensor")
    chip = position // CORES
    core = position % CORES
    core_pairs = [(p, p ^ 1) for p in range(shards)]

    def product(piece, shard, c):
        start = jnp.clip(shard, 0, chips - 1) * CORES + c
        part = lax.dynamic_slice_in_dim(weight, start * width, width, axis=1)
        return lax.dot_general(piece, part, (((1,), (1,)), ((), ())), preferred_element_type=f32)

    def both(piece, shard):
        other = lax.ppermute(piece, "tensor", core_pairs)
        return product(piece, shard, core) + product(other, shard, 1 - core)

    with jax.named_scope("expert"):
        total = both(own, chip)
        right = left = own
        for step in range(1, chips):
            right = lax.ppermute(right, "tensor", line_pairs(chips, [(i, i + 1) for i in range(step - 1, chips - 1)]))
            left = lax.ppermute(left, "tensor", line_pairs(chips, [(i, i - 1) for i in range(1, chips - step + 1)]))
            total = total + both(right, chip - step)
            total = total + both(left, chip + step)
        rows = total.astype(bf16)

    with jax.named_scope("return"):
        back = lax.all_to_all(rows, "expert", split_axis=0, concat_axis=0, tiled=True)

    with jax.named_scope("finish"):
        pick = (target[:, None] == jnp.arange(slots, dtype=jnp.int32)[None, :]).astype(bf16)
        returned = jnp.dot(pick, back, preferred_element_type=f32)
        grad_hidden = (gate_prob[:, None] * returned).astype(bf16)
        gate = jnp.sum(hidden_in.astype(f32) * returned, axis=1)
        gate = gate + lax.ppermute(gate, "tensor", core_pairs)
        turn = CORES
        while turn < shards:
            gate = gate + lax.ppermute(gate, "tensor", [(p, p ^ turn) for p in range(shards)])
            turn *= 2
    return grad_hidden, gate


def solution(mesh):
    return jax.shard_map(
        body,
        mesh=mesh,
        in_specs=(
            P("expert", "tensor"),
            P("expert", "tensor"),
            P("expert"),
            P("expert", None),
            P("expert", "tensor", None),
        ),
        out_specs=(P("expert", "tensor"), P("expert")),
        check_vma=False,
    )
```

```python
import functools

import jax
import jax.numpy as jnp
from jax import lax
from jax.experimental import pallas as pl
from jax.experimental.pallas import tpu as pltpu
from jax.sharding import PartitionSpec as P

SEGMENTS = 4
COLUMNS = 16
CORES = 2


def products(lists, chips, position_ref, *refs):
    count = 2 * chips - 1
    pieces, weight_ref = refs[: lists * count], refs[lists * count]
    mine_ref, other_ref, total = refs[lists * count + 1 :]
    rows, width = pieces[0].shape
    hidden = mine_ref.shape[1]
    position = position_ref[0]
    total[...] = jnp.zeros_like(total)
    for n in range(count):
        shard = position + chips - 1 - n

        @pl.when((shard >= 0) & (shard < chips))
        def _():
            part = weight_ref[:, pl.ds(pl.multiple_of(shard * width, 128), width)]
            for k in range(lists):
                total[k * rows : (k + 1) * rows, :] += lax.dot_general(
                    pieces[k * count + n][...], part, (((1,), (1,)), ((), ())), preferred_element_type=jnp.float32
                )

    mine_ref[...] = total[:, :hidden]
    other_ref[...] = total[:, hidden:]


def expert_rows(position, lists, weight, chips):
    rows = lists[0][0][2]
    width = lists[0][0][0].shape[1]
    hidden = weight.shape[0] // CORES
    arrays, specs = [], []
    for entries in lists:
        for array, first, _ in entries:
            arrays.append(array)
            specs.append(pl.BlockSpec((rows, width), functools.partial(lambda b, i: (b, 0), first // rows)))
    total = rows * len(lists)
    out = jax.ShapeDtypeStruct((total, hidden), jnp.float32)
    return pl.pallas_call(
        functools.partial(products, len(lists), chips),
        grid=(1,),
        out_shape=[out, out],
        in_specs=[pl.BlockSpec(memory_space=pltpu.SMEM)] + specs + [pl.BlockSpec(weight.shape, lambda i: (0, 0))],
        out_specs=[pl.BlockSpec((total, hidden), lambda i: (0, 0))] * 2,
        scratch_shapes=[pltpu.VMEM((total, CORES * hidden), jnp.float32)],
        compiler_params=pltpu.CompilerParams(vmem_limit_bytes=40 * 1024 * 1024),
        cost_estimate=pl.CostEstimate(
            flops=2 * total * weight.size, bytes_accessed=2 * weight.size + 2 * len(arrays) * rows * width, transcendentals=0
        ),
    )(position, *arrays, weight)


def body(grad_out, hidden_in, gate_prob, expert_ids, w_down):
    tokens, width = grad_out.shape
    groups = lax.axis_size("expert")
    shards = lax.axis_size("tensor")
    chips = shards // CORES
    experts = w_down.shape[0] * groups
    capacity = 2 * tokens // experts
    slots = experts * capacity
    block = COLUMNS * capacity
    half = block // 2
    weight = w_down[0]
    bf16, f32 = jnp.bfloat16, jnp.float32

    position = lax.axis_index("tensor")
    segment = lax.axis_index("expert") // COLUMNS
    chip, core = position // CORES, position % CORES
    core_pairs = [(p, p ^ 1) for p in range(shards)]
    length = SEGMENTS * chips

    def device(z, column, c):
        z = z % length
        return ((z // chips) * COLUMNS + column) * shards + (z % chips) * CORES + c

    def ring(way):
        return [
            (device(z, column, c), device(z + way, column, c))
            for z in range(length)
            for column in range(COLUMNS)
            for c in range(CORES)
        ]

    with jax.named_scope("route"):
        chosen = expert_ids[:, 0]
        onehot = (chosen[:, None] == jnp.arange(experts, dtype=jnp.int32)[None, :]).astype(bf16)
        row = jnp.arange(tokens, dtype=jnp.int32)
        before = (row[None, :] < row[:, None]).astype(bf16)
        counts = jnp.dot(before, onehot, preferred_element_type=f32)
        earlier = jnp.sum(counts * onehot.astype(f32), axis=1).astype(jnp.int32)
        target = chosen * capacity + earlier
        away = (chosen // COLUMNS - segment) % SEGMENTS
        sent_to = ((chosen % COLUMNS) * SEGMENTS + away) * capacity + earlier
        place = (jnp.arange(slots, dtype=jnp.int32)[:, None] == sent_to[None, :]).astype(bf16)
        send = jnp.dot(place, grad_out, preferred_element_type=f32).astype(bf16)

    with jax.named_scope("plane"):
        planes = [[s * COLUMNS + k for k in range(COLUMNS)] for s in range(SEGMENTS)]
        got = lax.all_to_all(send, "expert", split_axis=0, concat_axis=0, axis_index_groups=planes, tiled=True)
        got = got.reshape(COLUMNS, SEGMENTS, capacity, width)
        far = got[:, 2]
        right = jnp.concatenate([got[:, 0], got[:, 1], far[: COLUMNS // 2]], axis=0).reshape(-1, width)
        left = jnp.concatenate([got[:, 0], got[:, 3], far[COLUMNS // 2 :]], axis=0).reshape(-1, width)

    with jax.named_scope("weights"):
        def shards_of(c):
            return jnp.concatenate(
                [lax.dynamic_slice_in_dim(weight, (i * CORES + c) * width, width, axis=1) for i in range(chips)], axis=1
            )

        both = jnp.concatenate([shards_of(core), lax.ppermute(shards_of(1 - core), "tensor", core_pairs)], axis=0)
        where = chip.astype(jnp.int32).reshape(1)

    def finish_rows(pair):
        mine, other = pair
        return (mine + lax.ppermute(other, "tensor", core_pairs)).astype(bf16)

    with jax.named_scope("ring"):
        rights, lefts = [right], [left]
        steps = 3 * chips - 1
        for step in range(1, steps + 1):
            drop = block if step in (chips, 2 * chips) else 0
            right = lax.ppermute(right[drop:], ("expert", "tensor"), ring(1))
            left = lax.ppermute(left[drop:], ("expert", "tensor"), ring(-1))
            rights.append(right)
            lefts.append(left)
        first = {0: 0, 1: block, 2: 2 * block}

        def entry(array, which, rows):
            gone = right_rows - array.shape[0]
            return array, first[which] - gone, rows

        right_rows = 2 * block + half
        span = range(1, 2 * chips)
        own = [entry(lefts[chips - 1 - n], 0, block) for n in range(chips - 1)] + [
            entry(rights[n], 0, block) for n in range(chips)
        ]
        near = [[entry(rights[k], 1, block) for k in span], [entry(lefts[k], 1, block) for k in reversed(span)]]
        away2 = [
            [entry(rights[k + chips], 2, half) for k in span],
            [entry(lefts[k + chips], 2, half) for k in reversed(span)],
        ]
        own_rows = finish_rows(expert_rows(where, [own], both, chips))
        near_rows = finish_rows(expert_rows(where, near, both, chips))
        far_rows = finish_rows(expert_rows(where, away2, both, chips))
        around = jnp.concatenate([own_rows, near_rows[block:], far_rows, near_rows[:block]], axis=0)
        around = jnp.concatenate([around, around], axis=0)
        rows = lax.dynamic_slice_in_dim(around, ((SEGMENTS - segment) % SEGMENTS) * block, slots, axis=0)

    with jax.named_scope("return"):
        back = lax.all_to_all(rows, "expert", split_axis=0, concat_axis=0, tiled=True)

    with jax.named_scope("finish"):
        pick = (target[:, None] == jnp.arange(slots, dtype=jnp.int32)[None, :]).astype(bf16)
        returned = jnp.dot(pick, back, preferred_element_type=f32)
        grad_hidden = (gate_prob[:, None] * returned).astype(bf16)
        gate = jnp.sum(hidden_in.astype(f32) * returned, axis=1)
        gate = gate + lax.ppermute(gate, "tensor", core_pairs)
        turn = CORES
        while turn < shards:
            gate = gate + lax.ppermute(gate, "tensor", [(p, p ^ turn) for p in range(shards)])
            turn *= 2
    return grad_hidden, gate


def solution(mesh):
    return jax.shard_map(
        body,
        mesh=mesh,
        in_specs=(
            P("expert", "tensor"),
            P("expert", "tensor"),
            P("expert"),
            P("expert", None),
            P("expert", "tensor", None),
        ),
        out_specs=(P("expert", "tensor"), P("expert")),
        check_vma=False,
    )
```

```python
import functools

import jax
import jax.numpy as jnp
from jax import lax
from jax.experimental import pallas as pl
from jax.experimental.pallas import tpu as pltpu
from jax.sharding import PartitionSpec as P

CORES = 2
HALVES = 2
KINDS = 5


def line_shards(chip, chips):
    edge = (chip == 0) | (chip == chips - 1)
    shards = [chip, chip - 1, chip + 1, lax.rem(chip + 2, chips), chips - 1 - chip]
    valid = [chip >= 0, chip > 0, chip < chips - 1, chip >= 0, edge]
    return [jnp.clip(s, 0, chips - 1) for s in shards], valid


def near_kernel(chip_ref, *refs):
    kinds = KINDS - 1
    pieces, sources = refs[: HALVES * kinds], refs[HALVES * kinds : HALVES * kinds + CORES]
    out, tokens, weights, token_sems, weight_sems = refs[HALVES * kinds + CORES :]
    rows, width = pieces[0].shape
    hidden = weights.shape[1]
    shards, valid = line_shards(chip_ref[0], tokens.shape[1] // width)

    def token_copy(h, k):
        first = pl.multiple_of(shards[k] * width, 128)
        return pltpu.make_async_copy(
            pieces[h * kinds + k], tokens.at[pl.ds(h * rows, rows), pl.ds(first, width)], token_sems.at[h, k]
        )

    def weight_copy(n):
        return pltpu.make_async_copy(sources[n], weights.at[n], weight_sems.at[n])

    @pl.when(jnp.logical_not(valid[1] & valid[2]))
    def _():
        last = pl.multiple_of((tokens.shape[1] // width - 1 - chip_ref[0]) * width, 128)
        tokens[:, pl.ds(last, width)] = jnp.zeros((tokens.shape[0], width), tokens.dtype)

    for h in range(HALVES):
        weight_copy(h).start()
        for k in range(kinds):
            pl.when(valid[k])(token_copy(h, k).start)
    for h in range(HALVES):
        for k in range(kinds):
            pl.when(valid[k])(token_copy(h, k).wait)
    for n in range(CORES):
        weight_copy(n).wait()
        out[:, n * hidden : (n + 1) * hidden] = lax.dot_general(
            tokens[...], weights[n], (((1,), (1,)), ((), ())), preferred_element_type=jnp.float32
        )


def last_kernel(chips, chip_ref, total_ref, *refs):
    pieces, sources, out = refs[:HALVES], refs[HALVES : HALVES + CORES], refs[HALVES + CORES]
    weights, sems = refs[HALVES + CORES + 1 :]
    rows, width = pieces[0].shape
    hidden = weights.shape[1]
    shards, valid = line_shards(chip_ref[0], chips)
    first = pl.multiple_of(shards[-1] * width, 128)

    def weight_copy(n):
        return pltpu.make_async_copy(sources[n].at[:, pl.ds(first, width)], weights.at[n], sems.at[n])

    @pl.when(valid[-1])
    def _():
        for n in range(CORES):
            weight_copy(n).start()
        for n in range(CORES):
            weight_copy(n).wait()
            for h in range(HALVES):
                here = (slice(h * rows, (h + 1) * rows), slice(n * hidden, (n + 1) * hidden))
                more = lax.dot_general(
                    pieces[h][...], weights[n], (((1,), (1,)), ((), ())), preferred_element_type=jnp.float32
                )
                out[here] = (total_ref[here] + more).astype(out.dtype)

    @pl.when(jnp.logical_not(valid[-1]))
    def _():
        out[...] = total_ref[...].astype(out.dtype)


ANY = pl.BlockSpec(memory_space=pl.ANY)
SMEM = pl.BlockSpec(memory_space=pltpu.SMEM)
VMEM = pl.BlockSpec(memory_space=pltpu.VMEM)


def multiply_near(chip, pieces, weights):
    rows = pieces[0].shape[0] * HALVES
    hidden, depth = weights[0].shape
    return pl.pallas_call(
        near_kernel,
        out_shape=jax.ShapeDtypeStruct((rows, CORES * hidden), jnp.float32),
        in_specs=[SMEM] + [ANY] * (len(pieces) + CORES),
        out_specs=VMEM,
        scratch_shapes=[
            pltpu.VMEM((rows, depth), jnp.bfloat16),
            pltpu.VMEM((CORES, hidden, depth), jnp.bfloat16),
            pltpu.SemaphoreType.DMA((HALVES, KINDS)),
            pltpu.SemaphoreType.DMA((CORES,)),
        ],
        compiler_params=pltpu.CompilerParams(vmem_limit_bytes=32 * 1024 * 1024),
        cost_estimate=pl.CostEstimate(
            flops=2 * CORES * rows * hidden * depth, bytes_accessed=2 * (rows + CORES * hidden) * depth, transcendentals=0
        ),
    )(chip.reshape(1), *pieces, *weights)


def multiply_last(chip, chips, total, pieces, weights):
    width = pieces[0].shape[1]
    hidden = weights[0].shape[0]
    return pl.pallas_call(
        functools.partial(last_kernel, chips),
        out_shape=jax.ShapeDtypeStruct(total.shape, jnp.bfloat16),
        in_specs=[SMEM] + [VMEM] * (1 + len(pieces)) + [ANY] * CORES,
        out_specs=VMEM,
        scratch_shapes=[pltpu.VMEM((CORES, hidden, width), jnp.bfloat16), pltpu.SemaphoreType.DMA((CORES,))],
        compiler_params=pltpu.CompilerParams(vmem_limit_bytes=24 * 1024 * 1024),
        cost_estimate=pl.CostEstimate(
            flops=2 * total.size * width, bytes_accessed=8 * total.size, transcendentals=0
        ),
    )(chip.reshape(1), total, *pieces, *weights)


def place_kernel(to_ref, mine_ref, other_ref, out_ref):
    slots, tokens = out_ref.shape[0], mine_ref.shape[0]
    width = mine_ref.shape[1]
    core = to_ref[1:2, :]
    place = (lax.broadcasted_iota(jnp.int32, (slots, tokens), 0) == to_ref[0:1, :]).astype(jnp.bfloat16)
    mine = jnp.dot(place, mine_ref[...], preferred_element_type=jnp.float32).astype(jnp.bfloat16)
    other = jnp.dot(place, other_ref[...], preferred_element_type=jnp.float32).astype(jnp.bfloat16)
    first = core[:, :1] == 0
    out_ref[:, :width] = jnp.where(first, mine, other)
    out_ref[:, width:] = jnp.where(first, other, mine)


def body(grad_out, hidden_in, gate_prob, expert_ids, w_down):
    tokens, width = grad_out.shape
    groups = lax.axis_size("expert")
    shards = lax.axis_size("tensor")
    chips = shards // CORES
    experts = w_down.shape[0] * groups
    capacity = 2 * tokens // experts
    share = capacity // CORES
    slots = experts * capacity
    weight = w_down[0]
    hidden = weight.shape[0]
    bf16, f32 = jnp.bfloat16, jnp.float32

    position = lax.axis_index("tensor").astype(jnp.int32)
    chip, core = position // CORES, position % CORES
    core_pairs = [(p, p ^ 1) for p in range(shards)]

    def line(array, pairs):
        return lax.ppermute(array, "tensor", [(a * CORES + c, b * CORES + c) for a, b in pairs for c in range(CORES)])

    def swap(array):
        return lax.ppermute(array, "tensor", core_pairs)

    with jax.named_scope("route"):
        other_out = swap(grad_out)
        chosen = expert_ids[:, 0]
        onehot = (chosen[:, None] == jnp.arange(experts, dtype=jnp.int32)[None, :]).astype(bf16)
        row = jnp.arange(tokens, dtype=jnp.int32)
        before = (row[None, :] < row[:, None]).astype(bf16)
        counts = jnp.dot(before, onehot, preferred_element_type=f32)
        earlier = jnp.sum(counts * onehot.astype(f32), axis=1).astype(jnp.int32)
        away = jnp.where(earlier // share == core, 0, 1)
        target = away * (slots // CORES) + chosen * share + earlier % share
        sent_to = jnp.stack([target, jnp.full_like(target, core)])
        send = pl.pallas_call(
            place_kernel, out_shape=jax.ShapeDtypeStruct((slots // CORES, CORES * width), bf16)
        )(sent_to, grad_out, other_out)

    with jax.named_scope("weights"):
        other_weight = swap(weight)

    with jax.named_scope("dispatch"):
        got = lax.all_to_all(send, "expert", split_axis=0, concat_axis=0, tiled=True)

    with jax.named_scope("gather"):
        rows = got.shape[0] // HALVES
        own = [got[h * rows : (h + 1) * rows] for h in range(HALVES)]
        right1 = [line(x, [(0, 1), (1, 2), (2, 3)]) for x in own]
        left1 = [line(x, [(1, 0), (2, 1), (3, 2)]) for x in own]
        second = [line(r, [(1, 2), (2, 3)]) + line(l, [(2, 1), (1, 0)]) for r, l in zip(right1, left1)]
        third = [line(m, [(2, 3), (1, 0)]) for m in second]

    with jax.named_scope("products"):
        weights = [weight, other_weight]
        near = [x for h in range(HALVES) for x in (own[h], right1[h], left1[h], second[h])]
        total = multiply_near(chip, near, weights)
        filled = multiply_last(chip, chips, total, third, weights)

    with jax.named_scope("return"):
        back = lax.all_to_all(filled, "expert", split_axis=0, concat_axis=0, tiled=True)

    with jax.named_scope("finish"):
        back = jnp.concatenate([back[:, :hidden], swap(back[:, hidden:])], axis=0)
        pick = (target[:, None] == jnp.arange(slots, dtype=jnp.int32)[None, :]).astype(bf16)
        returned = jnp.dot(pick, back, preferred_element_type=f32)
        grad_hidden = (gate_prob[:, None] * returned).astype(bf16)
        part = jnp.sum(hidden_in.astype(f32) * returned, axis=1)
        parts = jnp.broadcast_to(part[None, :], (shards, tokens))
        gate = jnp.sum(lax.all_to_all(parts, "tensor", split_axis=0, concat_axis=0, tiled=True), axis=0)
    return grad_hidden, gate


def solution(mesh):
    return jax.shard_map(
        body,
        mesh=mesh,
        in_specs=(
            P("expert", "tensor"),
            P("expert", "tensor"),
            P("expert"),
            P("expert", None),
            P("expert", "tensor", None),
        ),
        out_specs=(P("expert", "tensor"), P("expert")),
        check_vma=False,
    )
```

```python
import functools

import jax
import jax.numpy as jnp
from jax import lax
from jax.experimental import pallas as pl
from jax.experimental.pallas import tpu as pltpu
from jax.sharding import PartitionSpec as P

CORES = 2
HALVES = 2
KINDS = 5


def line_shards(chip, chips):
    edge = (chip == 0) | (chip == chips - 1)
    shards = [chip, chip - 1, chip + 1, lax.rem(chip + 2, chips), chips - 1 - chip]
    valid = [chip >= 0, chip > 0, chip < chips - 1, chip >= 0, edge]
    return [jnp.clip(s, 0, chips - 1) for s in shards], valid


def near_kernel(place_ref, *refs):
    kinds = KINDS - 1
    count = HALVES * kinds
    pieces, sources = refs[:count], refs[count : count + CORES]
    out, tokens, weights, token_sems, weight_sems = refs[count + CORES :]
    width = pieces[0].shape[1]
    hidden = weights.shape[1]
    core = place_ref[1]
    shards, valid = line_shards(place_ref[0], tokens.shape[1] // (width * HALVES))

    def columns(h, k):
        block = shards[k] * HALVES + (core if h == 0 else 1 - core)
        return pl.ds(pl.multiple_of(block * width, 128), width)

    def token_copy(n):
        return pltpu.make_async_copy(pieces[n], tokens.at[:, columns(*divmod(n, kinds))], token_sems.at[n])

    def weight_copy(n):
        return pltpu.make_async_copy(sources[n], weights.at[n], weight_sems.at[n])

    @pl.when(valid[-1])
    def _():
        for h in range(HALVES):
            tokens[:, columns(h, KINDS - 1)] = jnp.zeros((tokens.shape[0], width), tokens.dtype)

    weight_copy(0).start()
    for n in range(count):
        pl.when(valid[n % kinds])(token_copy(n).start)
    weight_copy(1).start()
    for n in range(count):
        pl.when(valid[n % kinds])(token_copy(n).wait)
    for n in range(CORES):
        weight_copy(n).wait()
        out[:, n * hidden : (n + 1) * hidden] = lax.dot_general(
            tokens[...], weights[n], (((1,), (1,)), ((), ())), preferred_element_type=jnp.float32
        )


def last_kernel(chips, place_ref, total_ref, *refs):
    pieces, sources, out = refs[:HALVES], refs[HALVES : HALVES + CORES], refs[HALVES + CORES]
    weights, sems = refs[HALVES + CORES + 1 :]
    width = pieces[0].shape[1]
    hidden = weights.shape[2]
    core = place_ref[1]
    shards, valid = line_shards(place_ref[0], chips)

    def weight_copy(h, n):
        block = shards[-1] * HALVES + (core if h == 0 else 1 - core)
        part = sources[n].at[:, pl.ds(pl.multiple_of(block * width, 128), width)]
        return pltpu.make_async_copy(part, weights.at[h, n], sems.at[h, n])

    @pl.when(valid[-1])
    def _():
        for n in range(CORES):
            for h in range(HALVES):
                weight_copy(h, n).start()
        for n in range(CORES):
            here = slice(n * hidden, (n + 1) * hidden)
            more = total_ref[:, here]
            for h in range(HALVES):
                weight_copy(h, n).wait()
                more = more + lax.dot_general(
                    pieces[h][...], weights[h, n], (((1,), (1,)), ((), ())), preferred_element_type=jnp.float32
                )
            out[:, here] = more.astype(out.dtype)

    @pl.when(jnp.logical_not(valid[-1]))
    def _():
        out[...] = total_ref[...].astype(out.dtype)


HBM = pl.BlockSpec(memory_space=pltpu.HBM)
SMEM = pl.BlockSpec(memory_space=pltpu.SMEM)
VMEM = pl.BlockSpec(memory_space=pltpu.VMEM)


def multiply_near(where, pieces, weights):
    rows = pieces[0].shape[0]
    hidden, depth = weights[0].shape
    return pl.pallas_call(
        near_kernel,
        out_shape=jax.ShapeDtypeStruct((rows, CORES * hidden), jnp.float32),
        in_specs=[SMEM] + [HBM] * (len(pieces) + CORES),
        out_specs=VMEM,
        scratch_shapes=[
            pltpu.VMEM((rows, depth), jnp.bfloat16),
            pltpu.VMEM((CORES, hidden, depth), jnp.bfloat16),
            pltpu.SemaphoreType.DMA((HALVES * (KINDS - 1),)),
            pltpu.SemaphoreType.DMA((CORES,)),
        ],
        compiler_params=pltpu.CompilerParams(vmem_limit_bytes=32 * 1024 * 1024),
        cost_estimate=pl.CostEstimate(
            flops=2 * CORES * rows * hidden * depth, bytes_accessed=2 * (rows + CORES * hidden) * depth, transcendentals=0
        ),
    )(where, *pieces, *weights)


def multiply_last(where, chips, total, pieces, weights):
    width = pieces[0].shape[1]
    hidden = weights[0].shape[0]
    return pl.pallas_call(
        functools.partial(last_kernel, chips),
        out_shape=jax.ShapeDtypeStruct(total.shape, jnp.bfloat16),
        in_specs=[SMEM] + [VMEM] * (1 + HALVES) + [HBM] * CORES,
        out_specs=VMEM,
        scratch_shapes=[
            pltpu.VMEM((HALVES, CORES, hidden, width), jnp.bfloat16),
            pltpu.SemaphoreType.DMA((HALVES, CORES)),
        ],
        compiler_params=pltpu.CompilerParams(vmem_limit_bytes=24 * 1024 * 1024),
        cost_estimate=pl.CostEstimate(
            flops=2 * HALVES * total.size * width, bytes_accessed=8 * total.size, transcendentals=0
        ),
    )(where, total, *pieces, *weights)


def route_kernel(capacity, ids_ref, rows_ref, send_ref, target_ref):
    tokens = rows_ref.shape[0]
    slots = send_ref.shape[0]
    ids = ids_ref[...]
    chosen = (lax.broadcasted_iota(jnp.int32, (slots // capacity, tokens), 0) == ids).astype(jnp.float32)
    before = (
        lax.broadcasted_iota(jnp.int32, (tokens, tokens), 0) < lax.broadcasted_iota(jnp.int32, (tokens, tokens), 1)
    ).astype(jnp.bfloat16)
    counts = jnp.dot(chosen.astype(jnp.bfloat16), before, preferred_element_type=jnp.float32)
    earlier = jnp.sum(chosen * counts, axis=0, keepdims=True)
    target = ids * capacity + earlier.astype(jnp.int32)
    target_ref[...] = target
    place = (lax.broadcasted_iota(jnp.int32, (slots, tokens), 0) == target).astype(jnp.bfloat16)
    send_ref[...] = jnp.dot(place, rows_ref[...], preferred_element_type=jnp.float32).astype(send_ref.dtype)


def body(grad_out, hidden_in, gate_prob, expert_ids, w_down):
    tokens, width = grad_out.shape
    groups = lax.axis_size("expert")
    shards = lax.axis_size("tensor")
    chips = shards // CORES
    experts = w_down.shape[0] * groups
    capacity = 2 * tokens // experts
    share = capacity // CORES
    slots = experts * capacity
    weight = w_down[0]
    hidden = weight.shape[0]
    bf16, f32 = jnp.bfloat16, jnp.float32

    position = lax.axis_index("tensor").astype(jnp.int32)
    chip, core = position // CORES, position % CORES
    core_pairs = [(p, p ^ 1) for p in range(shards)]

    def line(array, pairs, flip=0):
        return lax.ppermute(
            array, "tensor", [(a * CORES + c, b * CORES + (c ^ flip)) for a, b in pairs for c in range(CORES)]
        )

    def swap(array):
        return lax.ppermute(array, "tensor", core_pairs)

    with jax.named_scope("route"):
        send, target = pl.pallas_call(
            functools.partial(route_kernel, capacity),
            out_shape=[jax.ShapeDtypeStruct((slots, width), bf16), jax.ShapeDtypeStruct((1, tokens), jnp.int32)],
        )(expert_ids.reshape(1, tokens), grad_out)

    with jax.named_scope("dispatch"):
        got = lax.all_to_all(send, "expert", split_axis=0, concat_axis=0, tiled=True)
        got = got.reshape(groups, CORES, share, width)

    with jax.named_scope("gather"):
        weights = [weight, swap(weight)]
        def part(c):
            return lax.dynamic_index_in_dim(got, c, axis=1, keepdims=False).reshape(groups * share, width)

        def gather(x, flip):
            right = line(x, [(0, 1), (1, 2), (2, 3)], flip)
            left = line(x, [(1, 0), (2, 1), (3, 2)], flip)
            second = line(right, [(1, 2), (2, 3)]) + line(left, [(2, 1), (1, 0)])
            return [swap(x) if flip else x, right, left, second, line(second, [(2, 3), (1, 0)])]

        halves = [gather(part(core), 0), gather(part(1 - core), 1)]

    with jax.named_scope("products"):
        where = jnp.stack([chip, core])
        total = multiply_near(where, halves[0][:-1] + halves[1][:-1], weights)
        filled = multiply_last(where, chips, total, [halves[0][-1], halves[1][-1]], weights)

    with jax.named_scope("return"):
        back = lax.all_to_all(filled, "expert", split_axis=0, concat_axis=0, tiled=True)

    with jax.named_scope("finish"):
        target = target.reshape(tokens)
        away = jnp.where(target % capacity // share == core, 0, 1)
        local = away * (slots // CORES) + target // capacity * share + target % share
        pick = (local[:, None] == jnp.arange(slots, dtype=jnp.int32)[None, :]).astype(bf16)
        back = jnp.concatenate([back[:, :hidden], swap(back[:, hidden:])], axis=0)
        returned = jnp.dot(pick, back, preferred_element_type=f32)
        grad_hidden = (gate_prob[:, None] * returned).astype(bf16)
        gate_part = jnp.sum(hidden_in.astype(f32) * returned, axis=1)
        parts = jnp.broadcast_to(gate_part[None, :], (shards, tokens))
        gate = jnp.sum(lax.all_to_all(parts, "tensor", split_axis=0, concat_axis=0, tiled=True), axis=0)
    return grad_hidden, gate


def solution(mesh):
    return jax.shard_map(
        body,
        mesh=mesh,
        in_specs=(
            P("expert", "tensor"),
            P("expert", "tensor"),
            P("expert"),
            P("expert", None),
            P("expert", "tensor", None),
        ),
        out_specs=(P("expert", "tensor"), P("expert")),
        check_vma=False,
    )
```

```python
import functools

import jax
import jax.numpy as jnp
from jax import lax
from jax.experimental import pallas as pl
from jax.experimental.pallas import tpu as pltpu
from jax.sharding import PartitionSpec as P

CORES = 2
HALVES = 2
KINDS = 5


def line_shards(chip, chips):
    steps = [0, -1, 1, -2, 2]
    shards = [chip + n for n in steps]
    return [jnp.clip(s, 0, chips - 1) for s in shards], [(s >= 0) & (s < chips) for s in shards]


def at_end(chip, chips):
    return (chip == 0) | (chip == chips - 1)


def near_kernel(place_ref, *refs):
    count = HALVES * KINDS
    pieces, sources = refs[:count], refs[count : count + CORES]
    out, tokens, weights, token_sems, weight_sems = refs[count + CORES :]
    width = pieces[0].shape[1]
    hidden = weights.shape[1]
    chip, core = place_ref[0], place_ref[1]
    chips = tokens.shape[1] // (width * HALVES)
    shards, valid = line_shards(chip, chips)

    def part(shard, h):
        block = shard * HALVES + (core if h == 0 else 1 - core)
        return pl.ds(pl.multiple_of(block * width, 128), width)

    def columns(h, k):
        return part(shards[k], h)

    def token_copy(n):
        return pltpu.make_async_copy(pieces[n], tokens.at[:, columns(*divmod(n, KINDS))], token_sems.at[n])

    def weight_copy(n):
        return pltpu.make_async_copy(sources[n], weights.at[n], weight_sems.at[n])

    @pl.when(at_end(chip, chips))
    def _():
        for h in range(HALVES):
            tokens[:, part(chips - 1 - chip, h)] = jnp.zeros((tokens.shape[0], width), tokens.dtype)

    weight_copy(0).start()
    for n in range(count):
        pl.when(valid[n % KINDS])(token_copy(n).start)
    weight_copy(1).start()
    for n in range(count):
        pl.when(valid[n % KINDS])(token_copy(n).wait)
    for n in range(CORES):
        weight_copy(n).wait()
        out[:, n * hidden : (n + 1) * hidden] = lax.dot_general(
            tokens[...], weights[n], (((1,), (1,)), ((), ())), preferred_element_type=jnp.float32
        )


def last_kernel(chips, place_ref, total_ref, *refs):
    pieces, sources = refs[: 2 * HALVES], refs[2 * HALVES : 2 * HALVES + CORES]
    out, weights, sems = refs[2 * HALVES + CORES :]
    width = pieces[0].shape[1]
    hidden = weights.shape[2]
    chip, core = place_ref[0], place_ref[1]
    end = at_end(chip, chips)

    def weight_copy(h, n):
        block = (chips - 1 - chip) * HALVES + (core if h == 0 else 1 - core)
        part = sources[n].at[:, pl.ds(pl.multiple_of(block * width, 128), width)]
        return pltpu.make_async_copy(part, weights.at[h, n], sems.at[h, n])

    @pl.when(end)
    def _():
        last = [jnp.where(chip == 0, pieces[2 * h + 1][...], pieces[2 * h][...]) for h in range(HALVES)]
        for n in range(CORES):
            for h in range(HALVES):
                weight_copy(h, n).start()
        for n in range(CORES):
            here = slice(n * hidden, (n + 1) * hidden)
            more = total_ref[:, here]
            for h in range(HALVES):
                weight_copy(h, n).wait()
                more = more + lax.dot_general(
                    last[h], weights[h, n], (((1,), (1,)), ((), ())), preferred_element_type=jnp.float32
                )
            out[:, here] = more.astype(out.dtype)

    @pl.when(jnp.logical_not(end))
    def _():
        out[...] = total_ref[...].astype(out.dtype)


HBM = pl.BlockSpec(memory_space=pltpu.HBM)
SMEM = pl.BlockSpec(memory_space=pltpu.SMEM)
VMEM = pl.BlockSpec(memory_space=pltpu.VMEM)


def multiply_near(where, pieces, weights):
    rows = pieces[0].shape[0]
    hidden, depth = weights[0].shape
    return pl.pallas_call(
        near_kernel,
        out_shape=jax.ShapeDtypeStruct((rows, CORES * hidden), jnp.float32),
        in_specs=[SMEM] + [HBM] * (len(pieces) + CORES),
        out_specs=VMEM,
        scratch_shapes=[
            pltpu.VMEM((rows, depth), jnp.bfloat16),
            pltpu.VMEM((CORES, hidden, depth), jnp.bfloat16),
            pltpu.SemaphoreType.DMA((HALVES * KINDS,)),
            pltpu.SemaphoreType.DMA((CORES,)),
        ],
        compiler_params=pltpu.CompilerParams(vmem_limit_bytes=32 * 1024 * 1024),
        cost_estimate=pl.CostEstimate(
            flops=2 * CORES * rows * hidden * depth, bytes_accessed=2 * (rows + CORES * hidden) * depth, transcendentals=0
        ),
    )(where, *pieces, *weights)


def multiply_last(where, chips, total, pieces, weights):
    width = pieces[0].shape[1]
    hidden = weights[0].shape[0]
    return pl.pallas_call(
        functools.partial(last_kernel, chips),
        out_shape=jax.ShapeDtypeStruct(total.shape, jnp.bfloat16),
        in_specs=[SMEM] + [VMEM] * (1 + 2 * HALVES) + [HBM] * CORES,
        out_specs=VMEM,
        scratch_shapes=[
            pltpu.VMEM((HALVES, CORES, hidden, width), jnp.bfloat16),
            pltpu.SemaphoreType.DMA((HALVES, CORES)),
        ],
        compiler_params=pltpu.CompilerParams(vmem_limit_bytes=24 * 1024 * 1024),
        cost_estimate=pl.CostEstimate(
            flops=2 * HALVES * total.size * width, bytes_accessed=8 * total.size, transcendentals=0
        ),
    )(where, total, *pieces, *weights)


def route_kernel(capacity, ids_ref, rows_ref, send_ref, target_ref):
    tokens = rows_ref.shape[0]
    slots = send_ref.shape[0]
    ids = ids_ref[...]
    chosen = (lax.broadcasted_iota(jnp.int32, (slots // capacity, tokens), 0) == ids).astype(jnp.float32)
    before = (
        lax.broadcasted_iota(jnp.int32, (tokens, tokens), 0) < lax.broadcasted_iota(jnp.int32, (tokens, tokens), 1)
    ).astype(jnp.bfloat16)
    counts = jnp.dot(chosen.astype(jnp.bfloat16), before, preferred_element_type=jnp.float32)
    earlier = jnp.sum(chosen * counts, axis=0, keepdims=True)
    target = ids * capacity + earlier.astype(jnp.int32)
    target_ref[...] = target
    place = (lax.broadcasted_iota(jnp.int32, (slots, tokens), 0) == target).astype(jnp.bfloat16)
    send_ref[...] = jnp.dot(place, rows_ref[...], preferred_element_type=jnp.float32).astype(send_ref.dtype)


def finish_kernel(shards, local_ref, gate_ref, back_ref, across_ref, hidden_ref, grad_ref, parts_ref):
    tokens, hidden = hidden_ref.shape
    slots = back_ref.shape[0]

    def column(row):
        return jnp.broadcast_to(row, (128, tokens)).T

    def wide(array, width):
        return jnp.concatenate([array] * (width // 128), axis=1)

    local = wide(column(local_ref[...].astype(jnp.float32)).astype(jnp.int32), slots)
    slot = lax.broadcasted_iota(jnp.int32, (tokens, slots), 1)
    mine = (local == slot).astype(jnp.bfloat16)
    other = (local == slot + slots).astype(jnp.bfloat16)
    returned = jnp.dot(mine, back_ref[...], preferred_element_type=jnp.float32)
    returned = returned + jnp.dot(other, across_ref[...], preferred_element_type=jnp.float32)
    grad_ref[...] = (wide(column(gate_ref[...]), hidden) * returned).astype(grad_ref.dtype)
    product = hidden_ref[...].astype(jnp.float32) * returned
    folded = sum(product[:, n * 128 : (n + 1) * 128] for n in range(hidden // 128))
    part = jnp.sum(folded.T, axis=0, keepdims=True)
    parts_ref[...] = jnp.broadcast_to(part, (shards, tokens))


def finish(local, gate_prob, back, across, hidden_in, shards):
    tokens, hidden = hidden_in.shape
    slots = back.shape[0]
    steps = 2
    step = tokens // steps
    row = pl.BlockSpec((1, step), lambda i: (0, i))
    rows = pl.BlockSpec((step, hidden), lambda i: (i, 0))
    whole = pl.BlockSpec((slots, hidden), lambda i: (0, 0))
    return pl.pallas_call(
        functools.partial(finish_kernel, shards),
        grid=(steps,),
        out_shape=[
            jax.ShapeDtypeStruct((tokens, hidden), jnp.bfloat16),
            jax.ShapeDtypeStruct((shards, tokens), jnp.float32),
        ],
        in_specs=[row, row, whole, whole, rows],
        out_specs=[rows, pl.BlockSpec((shards, step), lambda i: (0, i))],
        compiler_params=pltpu.CompilerParams(vmem_limit_bytes=24 * 1024 * 1024),
        cost_estimate=pl.CostEstimate(
            flops=4 * tokens * hidden * slots, bytes_accessed=8 * tokens * hidden, transcendentals=0
        ),
    )(local, gate_prob.reshape(1, tokens), back, across, hidden_in)


def body(grad_out, hidden_in, gate_prob, expert_ids, w_down):
    tokens, width = grad_out.shape
    groups = lax.axis_size("expert")
    shards = lax.axis_size("tensor")
    chips = shards // CORES
    experts = w_down.shape[0] * groups
    capacity = 2 * tokens // experts
    share = capacity // CORES
    slots = experts * capacity
    weight = w_down[0]
    hidden = weight.shape[0]
    bf16, f32 = jnp.bfloat16, jnp.float32

    position = lax.axis_index("tensor").astype(jnp.int32)
    chip, core = position // CORES, position % CORES
    core_pairs = [(p, p ^ 1) for p in range(shards)]

    def line(array, pairs, flip=0):
        return lax.ppermute(
            array, "tensor", [(a * CORES + c, b * CORES + (c ^ flip)) for a, b in pairs for c in range(CORES)]
        )

    def swap(array):
        return lax.ppermute(array, "tensor", core_pairs)

    with jax.named_scope("route"):
        send, target = pl.pallas_call(
            functools.partial(route_kernel, capacity),
            out_shape=[jax.ShapeDtypeStruct((slots, width), bf16), jax.ShapeDtypeStruct((1, tokens), jnp.int32)],
        )(expert_ids.reshape(1, tokens), grad_out)

    with jax.named_scope("dispatch"):
        got = lax.all_to_all(send, "expert", split_axis=0, concat_axis=0, tiled=True)
        got = got.reshape(groups, CORES, share, width)

    with jax.named_scope("gather"):
        weights = [weight, swap(weight)]
        def part(c):
            return lax.dynamic_index_in_dim(got, c, axis=1, keepdims=False).reshape(groups * share, width)

        def gather(x, flip):
            right = line(x, [(0, 1), (1, 2), (2, 3)], flip)
            left = line(x, [(1, 0), (2, 1), (3, 2)], flip)
            right2 = line(right, [(1, 2), (2, 3)])
            left2 = line(left, [(2, 1), (1, 0)])
            last = [line(right2, [(2, 3)]), line(left2, [(1, 0)])]
            return [swap(x) if flip else x, right, left, right2, left2], last

        (near, last), (crossed, crossed_last) = gather(part(core), 0), gather(part(1 - core), 1)

    with jax.named_scope("products"):
        where = jnp.stack([chip, core])
        total = multiply_near(where, near + crossed, weights)
        filled = multiply_last(where, chips, total, last + crossed_last, weights)

    with jax.named_scope("return"):
        back = lax.all_to_all(filled, "expert", split_axis=0, concat_axis=0, tiled=True)

    with jax.named_scope("finish"):
        share_of = target % capacity // share
        local = jnp.where(share_of == core, 0, slots // CORES) + target // capacity * share + target % share
        across = swap(back[:, hidden:])
        grad_hidden, parts = finish(local, gate_prob, back, across, hidden_in, shards)
        gate = jnp.sum(lax.all_to_all(parts, "tensor", split_axis=0, concat_axis=0, tiled=True), axis=0)
    return grad_hidden, gate


def solution(mesh):
    return jax.shard_map(
        body,
        mesh=mesh,
        in_specs=(
            P("expert", "tensor"),
            P("expert", "tensor"),
            P("expert"),
            P("expert", None),
            P("expert", "tensor", None),
        ),
        out_specs=(P("expert", "tensor"), P("expert")),
        check_vma=False,
    )
```

```python
import functools

import jax
import jax.numpy as jnp
from jax import lax
from jax.experimental import pallas as pl
from jax.experimental.pallas import tpu as pltpu
from jax.sharding import PartitionSpec as P

CORES = 2
HALVES = 2
KINDS = 5


def line_shards(chip, chips):
    steps = [0, -1, 1, -2, 2]
    shards = [chip + n for n in steps]
    return [jnp.clip(s, 0, chips - 1) for s in shards], [(s >= 0) & (s < chips) for s in shards]


def at_end(chip, chips):
    return (chip == 0) | (chip == chips - 1)


def near_kernel(place_ref, *refs):
    count = HALVES * KINDS
    pieces, sources = refs[:count], refs[count : count + CORES]
    out, tokens, weights, token_sems, weight_sems = refs[count + CORES :]
    width = pieces[0].shape[1]
    hidden = weights.shape[1]
    chip, core = place_ref[0], place_ref[1]
    chips = tokens.shape[1] // (width * HALVES)
    shards, valid = line_shards(chip, chips)

    def part(shard, h):
        block = shard * HALVES + (core if h == 0 else 1 - core)
        return pl.ds(pl.multiple_of(block * width, 128), width)

    def columns(h, k):
        return part(shards[k], h)

    def token_copy(n):
        return pltpu.make_async_copy(pieces[n], tokens.at[:, columns(*divmod(n, KINDS))], token_sems.at[n])

    def weight_copy(n):
        return pltpu.make_async_copy(sources[n], weights.at[n], weight_sems.at[n])

    @pl.when(at_end(chip, chips))
    def _():
        for h in range(HALVES):
            tokens[:, part(chips - 1 - chip, h)] = jnp.zeros((tokens.shape[0], width), tokens.dtype)

    weight_copy(0).start()
    for n in range(count):
        pl.when(valid[n % KINDS])(token_copy(n).start)
    weight_copy(1).start()
    for n in range(count):
        pl.when(valid[n % KINDS])(token_copy(n).wait)
    for n in range(CORES):
        weight_copy(n).wait()
        out[:, n * hidden : (n + 1) * hidden] = lax.dot_general(
            tokens[...], weights[n], (((1,), (1,)), ((), ())), preferred_element_type=jnp.float32
        )


def last_kernel(chips, place_ref, total_ref, *refs):
    pieces, sources = refs[: 2 * HALVES], refs[2 * HALVES : 2 * HALVES + CORES]
    out, weights, sems = refs[2 * HALVES + CORES :]
    width = pieces[0].shape[1]
    hidden = weights.shape[2]
    chip, core = place_ref[0], place_ref[1]
    end = at_end(chip, chips)

    def weight_copy(h, n):
        block = (chips - 1 - chip) * HALVES + (core if h == 0 else 1 - core)
        part = sources[n].at[:, pl.ds(pl.multiple_of(block * width, 128), width)]
        return pltpu.make_async_copy(part, weights.at[h, n], sems.at[h, n])

    @pl.when(end)
    def _():
        last = [jnp.where(chip == 0, pieces[2 * h + 1][...], pieces[2 * h][...]) for h in range(HALVES)]
        for n in range(CORES):
            for h in range(HALVES):
                weight_copy(h, n).start()
        for n in range(CORES):
            here = slice(n * hidden, (n + 1) * hidden)
            more = total_ref[:, here]
            for h in range(HALVES):
                weight_copy(h, n).wait()
                more = more + lax.dot_general(
                    last[h], weights[h, n], (((1,), (1,)), ((), ())), preferred_element_type=jnp.float32
                )
            out[:, here] = more.astype(out.dtype)

    @pl.when(jnp.logical_not(end))
    def _():
        out[...] = total_ref[...].astype(out.dtype)


HBM = pl.BlockSpec(memory_space=pltpu.HBM)
SMEM = pl.BlockSpec(memory_space=pltpu.SMEM)
VMEM = pl.BlockSpec(memory_space=pltpu.VMEM)


def multiply_near(where, pieces, weights):
    rows = pieces[0].shape[0]
    hidden, depth = weights[0].shape
    return pl.pallas_call(
        near_kernel,
        out_shape=jax.ShapeDtypeStruct((rows, CORES * hidden), jnp.float32),
        in_specs=[SMEM] + [HBM] * (len(pieces) + CORES),
        out_specs=VMEM,
        scratch_shapes=[
            pltpu.VMEM((rows, depth), jnp.bfloat16),
            pltpu.VMEM((CORES, hidden, depth), jnp.bfloat16),
            pltpu.SemaphoreType.DMA((HALVES * KINDS,)),
            pltpu.SemaphoreType.DMA((CORES,)),
        ],
        compiler_params=pltpu.CompilerParams(vmem_limit_bytes=32 * 1024 * 1024),
        cost_estimate=pl.CostEstimate(
            flops=2 * CORES * rows * hidden * depth, bytes_accessed=2 * (rows + CORES * hidden) * depth, transcendentals=0
        ),
    )(where, *pieces, *weights)


def multiply_last(where, chips, total, pieces, weights):
    width = pieces[0].shape[1]
    hidden = weights[0].shape[0]
    return pl.pallas_call(
        functools.partial(last_kernel, chips),
        out_shape=jax.ShapeDtypeStruct(total.shape, jnp.bfloat16),
        in_specs=[SMEM] + [VMEM] * (1 + 2 * HALVES) + [HBM] * CORES,
        out_specs=VMEM,
        scratch_shapes=[
            pltpu.VMEM((HALVES, CORES, hidden, width), jnp.bfloat16),
            pltpu.SemaphoreType.DMA((HALVES, CORES)),
        ],
        compiler_params=pltpu.CompilerParams(vmem_limit_bytes=24 * 1024 * 1024),
        cost_estimate=pl.CostEstimate(
            flops=2 * HALVES * total.size * width, bytes_accessed=8 * total.size, transcendentals=0
        ),
    )(where, total, *pieces, *weights)


def route_kernel(capacity, ids_ref, rows_ref, send_ref, target_ref, slot_ref):
    tokens = rows_ref.shape[0]
    block = send_ref.shape[0]
    experts = block * HALVES // capacity

    @pl.when(pl.program_id(0) == 0)
    def _():
        ids = ids_ref[...]
        chosen = (lax.broadcasted_iota(jnp.int32, (experts, tokens), 0) == ids).astype(jnp.float32)
        before = (
            lax.broadcasted_iota(jnp.int32, (tokens, tokens), 0) < lax.broadcasted_iota(jnp.int32, (tokens, tokens), 1)
        ).astype(jnp.bfloat16)
        counts = jnp.dot(chosen.astype(jnp.bfloat16), before, preferred_element_type=jnp.float32)
        earlier = jnp.sum(chosen * counts, axis=0, keepdims=True)
        slot_ref[...] = ids * capacity + earlier.astype(jnp.int32)
        target_ref[...] = slot_ref[...]

    first = pl.program_id(0) * block
    place = (lax.broadcasted_iota(jnp.int32, (block, tokens), 0) == slot_ref[...] - first).astype(jnp.bfloat16)
    send_ref[...] = jnp.dot(place, rows_ref[...], preferred_element_type=jnp.float32).astype(send_ref.dtype)


def finish_kernel(shards, local_ref, gate_ref, back_ref, across_ref, hidden_ref, grad_ref, parts_ref):
    tokens, hidden = hidden_ref.shape
    slots = back_ref.shape[0]

    def column(row):
        return jnp.broadcast_to(row, (128, tokens)).T

    def wide(array, width):
        return jnp.concatenate([array] * (width // 128), axis=1)

    local = wide(column(local_ref[...].astype(jnp.float32)).astype(jnp.int32), slots)
    slot = lax.broadcasted_iota(jnp.int32, (tokens, slots), 1)
    mine = (local == slot).astype(jnp.bfloat16)
    other = (local == slot + slots).astype(jnp.bfloat16)
    returned = jnp.dot(mine, back_ref[...], preferred_element_type=jnp.float32)
    returned = returned + jnp.dot(other, across_ref[...], preferred_element_type=jnp.float32)
    grad_ref[...] = (wide(column(gate_ref[...]), hidden) * returned).astype(grad_ref.dtype)
    product = hidden_ref[...].astype(jnp.float32) * returned
    folded = sum(product[:, n * 128 : (n + 1) * 128] for n in range(hidden // 128))
    part = jnp.sum(folded.T, axis=0, keepdims=True)
    parts_ref[...] = jnp.broadcast_to(part, (shards, tokens))


def finish(local, gate_prob, back, across, hidden_in, shards):
    tokens, hidden = hidden_in.shape
    slots = back.shape[0]
    steps = 2
    step = tokens // steps
    row = pl.BlockSpec((1, step), lambda i: (0, i))
    rows = pl.BlockSpec((step, hidden), lambda i: (i, 0))
    whole = pl.BlockSpec((slots, hidden), lambda i: (0, 0))
    return pl.pallas_call(
        functools.partial(finish_kernel, shards),
        grid=(steps,),
        out_shape=[
            jax.ShapeDtypeStruct((tokens, hidden), jnp.bfloat16),
            jax.ShapeDtypeStruct((shards, tokens), jnp.float32),
        ],
        in_specs=[row, row, whole, whole, rows],
        out_specs=[rows, pl.BlockSpec((shards, step), lambda i: (0, i))],
        compiler_params=pltpu.CompilerParams(vmem_limit_bytes=24 * 1024 * 1024),
        cost_estimate=pl.CostEstimate(
            flops=4 * tokens * hidden * slots, bytes_accessed=8 * tokens * hidden, transcendentals=0
        ),
    )(local, gate_prob.reshape(1, tokens), back, across, hidden_in)


def body(grad_out, hidden_in, gate_prob, expert_ids, w_down):
    tokens, width = grad_out.shape
    groups = lax.axis_size("expert")
    shards = lax.axis_size("tensor")
    chips = shards // CORES
    experts = w_down.shape[0] * groups
    capacity = 2 * tokens // experts
    share = capacity // CORES
    slots = experts * capacity
    weight = w_down[0]
    hidden = weight.shape[0]
    bf16, f32 = jnp.bfloat16, jnp.float32

    position = lax.axis_index("tensor").astype(jnp.int32)
    chip, core = position // CORES, position % CORES
    core_pairs = [(p, p ^ 1) for p in range(shards)]

    def line(array, pairs, flip=0):
        return lax.ppermute(
            array, "tensor", [(a * CORES + c, b * CORES + (c ^ flip)) for a, b in pairs for c in range(CORES)]
        )

    def swap(array):
        return lax.ppermute(array, "tensor", core_pairs)

    with jax.named_scope("route"):
        send, target = pl.pallas_call(
            functools.partial(route_kernel, capacity),
            grid=(HALVES,),
            out_shape=[jax.ShapeDtypeStruct((slots, width), bf16), jax.ShapeDtypeStruct((1, tokens), jnp.int32)],
            in_specs=[pl.BlockSpec((1, tokens), lambda i: (0, 0)), pl.BlockSpec((tokens, width), lambda i: (0, 0))],
            out_specs=[
                pl.BlockSpec((slots // HALVES, width), lambda i: (i, 0)),
                pl.BlockSpec((1, tokens), lambda i: (0, 0)),
            ],
            scratch_shapes=[pltpu.VMEM((1, tokens), jnp.int32)],
        )(expert_ids.reshape(1, tokens), grad_out)

    with jax.named_scope("dispatch"):
        got = lax.all_to_all(send, "expert", split_axis=0, concat_axis=0, tiled=True)
        got = got.reshape(groups, CORES, share, width)

    with jax.named_scope("gather"):
        weights = [weight, swap(weight)]
        def part(c):
            return lax.dynamic_index_in_dim(got, c, axis=1, keepdims=False).reshape(groups * share, width)

        def gather(x, flip):
            right = line(x, [(0, 1), (1, 2), (2, 3)], flip)
            left = line(x, [(1, 0), (2, 1), (3, 2)], flip)
            right2 = line(right, [(1, 2), (2, 3)])
            left2 = line(left, [(2, 1), (1, 0)])
            last = [line(right2, [(2, 3)]), line(left2, [(1, 0)])]
            return [swap(x) if flip else x, right, left, right2, left2], last

        (near, last), (crossed, crossed_last) = gather(part(core), 0), gather(part(1 - core), 1)

    with jax.named_scope("products"):
        where = jnp.stack([chip, core])
        total = multiply_near(where, near + crossed, weights)
        filled = multiply_last(where, chips, total, last + crossed_last, weights)

    with jax.named_scope("return"):
        back = lax.all_to_all(filled, "expert", split_axis=0, concat_axis=0, tiled=True)

    with jax.named_scope("finish"):
        share_of = target % capacity // share
        local = jnp.where(share_of == core, 0, slots // CORES) + target // capacity * share + target % share
        across = swap(back[:, hidden:])
        grad_hidden, parts = finish(local, gate_prob, back, across, hidden_in, shards)
        gate = jnp.sum(lax.all_to_all(parts, "tensor", split_axis=0, concat_axis=0, tiled=True), axis=0)
    return grad_hidden, gate


def solution(mesh):
    return jax.shard_map(
        body,
        mesh=mesh,
        in_specs=(
            P("expert", "tensor"),
            P("expert", "tensor"),
            P("expert"),
            P("expert", None),
            P("expert", "tensor", None),
        ),
        out_specs=(P("expert", "tensor"), P("expert")),
        check_vma=False,
    )
```

```python
import functools

import jax
import jax.numpy as jnp
from jax import lax
from jax.experimental import pallas as pl
from jax.experimental.pallas import tpu as pltpu
from jax.sharding import PartitionSpec as P

CORES = 2
HALVES = 2
KINDS = 5


def line_shards(chip, chips):
    steps = [0, -1, 1, -2, 2]
    shards = [chip + n for n in steps]
    return [jnp.clip(s, 0, chips - 1) for s in shards], [(s >= 0) & (s < chips) for s in shards]


def at_end(chip, chips):
    return (chip == 0) | (chip == chips - 1)


def near_kernel(place_ref, *refs):
    count = HALVES * KINDS
    pieces, sources = refs[:count], refs[count : count + CORES]
    out, tokens, weights, token_sems, weight_sems = refs[count + CORES :]
    width = pieces[0].shape[1]
    hidden = weights.shape[1]
    chip, core = place_ref[0], place_ref[1]
    chips = tokens.shape[1] // (width * HALVES)
    shards, valid = line_shards(chip, chips)

    def part(shard, h):
        block = shard * HALVES + (core if h == 0 else 1 - core)
        return pl.ds(pl.multiple_of(block * width, 128), width)

    def columns(h, k):
        return part(shards[k], h)

    def token_copy(n):
        return pltpu.make_async_copy(pieces[n], tokens.at[:, columns(*divmod(n, KINDS))], token_sems.at[n])

    def weight_copy(n):
        return pltpu.make_async_copy(sources[n], weights.at[n], weight_sems.at[n])

    @pl.when(at_end(chip, chips))
    def _():
        for h in range(HALVES):
            tokens[:, part(chips - 1 - chip, h)] = jnp.zeros((tokens.shape[0], width), tokens.dtype)

    weight_copy(0).start()
    for n in range(count):
        pl.when(valid[n % KINDS])(token_copy(n).start)
    weight_copy(1).start()
    for n in range(count):
        pl.when(valid[n % KINDS])(token_copy(n).wait)
    for n in range(CORES):
        weight_copy(n).wait()
        out[:, n * hidden : (n + 1) * hidden] = lax.dot_general(
            tokens[...], weights[n], (((1,), (1,)), ((), ())), preferred_element_type=jnp.float32
        )


def last_kernel(chips, place_ref, total_ref, *refs):
    pieces, sources = refs[: 2 * HALVES], refs[2 * HALVES : 2 * HALVES + CORES]
    out, weights, sems = refs[2 * HALVES + CORES :]
    width = pieces[0].shape[1]
    hidden = weights.shape[2]
    chip, core = place_ref[0], place_ref[1]
    end = at_end(chip, chips)

    def weight_copy(h, n):
        block = (chips - 1 - chip) * HALVES + (core if h == 0 else 1 - core)
        part = sources[n].at[:, pl.ds(pl.multiple_of(block * width, 128), width)]
        return pltpu.make_async_copy(part, weights.at[h, n], sems.at[h, n])

    step = pl.program_id(0)

    @pl.when(end & (step == 0))
    def _():
        for n in range(CORES):
            for h in range(HALVES):
                weight_copy(h, n).start()

    for n in range(CORES):

        @pl.when(end & (step == n))
        def _():
            more = total_ref[...]
            for h in range(HALVES):
                last = jnp.where(chip == 0, pieces[2 * h + 1][...], pieces[2 * h][...])
                weight_copy(h, n).wait()
                more = more + lax.dot_general(
                    last, weights[h, n], (((1,), (1,)), ((), ())), preferred_element_type=jnp.float32
                )
            out[...] = more.astype(out.dtype)

    @pl.when(jnp.logical_not(end))
    def _():
        out[...] = total_ref[...].astype(out.dtype)


HBM = pl.BlockSpec(memory_space=pltpu.HBM)
SMEM = pl.BlockSpec(memory_space=pltpu.SMEM)
VMEM = pl.BlockSpec(memory_space=pltpu.VMEM)


def multiply_near(where, pieces, weights):
    rows = pieces[0].shape[0]
    hidden, depth = weights[0].shape
    return pl.pallas_call(
        near_kernel,
        out_shape=jax.ShapeDtypeStruct((rows, CORES * hidden), jnp.float32),
        in_specs=[SMEM] + [HBM] * (len(pieces) + CORES),
        out_specs=VMEM,
        scratch_shapes=[
            pltpu.VMEM((rows, depth), jnp.bfloat16),
            pltpu.VMEM((CORES, hidden, depth), jnp.bfloat16),
            pltpu.SemaphoreType.DMA((HALVES * KINDS,)),
            pltpu.SemaphoreType.DMA((CORES,)),
        ],
        compiler_params=pltpu.CompilerParams(vmem_limit_bytes=32 * 1024 * 1024),
        cost_estimate=pl.CostEstimate(
            flops=2 * CORES * rows * hidden * depth, bytes_accessed=2 * (rows + CORES * hidden) * depth, transcendentals=0
        ),
    )(where, *pieces, *weights)


def multiply_last(where, chips, total, pieces, weights):
    rows, width = pieces[0].shape
    hidden = weights[0].shape[0]
    return pl.pallas_call(
        functools.partial(last_kernel, chips),
        out_shape=jax.ShapeDtypeStruct(total.shape, jnp.bfloat16),
        grid=(CORES,),
        in_specs=[SMEM, pl.BlockSpec((rows, hidden), lambda n: (0, n))]
        + [pl.BlockSpec((rows, width), lambda n: (0, 0))] * (2 * HALVES)
        + [HBM] * CORES,
        out_specs=pl.BlockSpec((rows, hidden), lambda n: (0, n)),
        scratch_shapes=[
            pltpu.VMEM((HALVES, CORES, hidden, width), jnp.bfloat16),
            pltpu.SemaphoreType.DMA((HALVES, CORES)),
        ],
        compiler_params=pltpu.CompilerParams(vmem_limit_bytes=24 * 1024 * 1024),
        cost_estimate=pl.CostEstimate(
            flops=2 * HALVES * total.size * width, bytes_accessed=8 * total.size, transcendentals=0
        ),
    )(where, total, *pieces, *weights)


def route_kernel(capacity, ids_ref, rows_ref, send_ref, target_ref):
    tokens = rows_ref.shape[0]
    slots = send_ref.shape[0]
    ids = ids_ref[...]
    chosen = (lax.broadcasted_iota(jnp.int32, (slots // capacity, tokens), 0) == ids).astype(jnp.float32)
    before = (
        lax.broadcasted_iota(jnp.int32, (tokens, tokens), 0) < lax.broadcasted_iota(jnp.int32, (tokens, tokens), 1)
    ).astype(jnp.bfloat16)
    counts = jnp.dot(chosen.astype(jnp.bfloat16), before, preferred_element_type=jnp.float32)
    earlier = jnp.sum(chosen * counts, axis=0, keepdims=True)
    target = ids * capacity + earlier.astype(jnp.int32)
    target_ref[...] = target
    place = (lax.broadcasted_iota(jnp.int32, (slots, tokens), 0) == target).astype(jnp.bfloat16)
    send_ref[...] = jnp.dot(place, rows_ref[...], preferred_element_type=jnp.float32).astype(send_ref.dtype)


def finish_kernel(shards, local_ref, gate_ref, back_ref, across_ref, hidden_ref, grad_ref, parts_ref):
    tokens, hidden = hidden_ref.shape
    slots = back_ref.shape[0]

    def column(row):
        return jnp.broadcast_to(row, (128, tokens)).T

    def wide(array, width):
        return jnp.concatenate([array] * (width // 128), axis=1)

    local = wide(column(local_ref[...].astype(jnp.float32)).astype(jnp.int32), slots)
    slot = lax.broadcasted_iota(jnp.int32, (tokens, slots), 1)
    mine = (local == slot).astype(jnp.bfloat16)
    other = (local == slot + slots).astype(jnp.bfloat16)
    returned = jnp.dot(mine, back_ref[...], preferred_element_type=jnp.float32)
    returned = returned + jnp.dot(other, across_ref[...], preferred_element_type=jnp.float32)
    grad_ref[...] = (wide(column(gate_ref[...]), hidden) * returned).astype(grad_ref.dtype)
    product = hidden_ref[...].astype(jnp.float32) * returned
    folded = sum(product[:, n * 128 : (n + 1) * 128] for n in range(hidden // 128))
    part = jnp.sum(folded.T, axis=0, keepdims=True)
    parts_ref[...] = jnp.broadcast_to(part, (shards, tokens))


def finish(local, gate_prob, back, across, hidden_in, shards):
    tokens, hidden = hidden_in.shape
    slots = back.shape[0]
    steps = 2
    step = tokens // steps
    row = pl.BlockSpec((1, step), lambda i: (0, i))
    rows = pl.BlockSpec((step, hidden), lambda i: (i, 0))
    whole = pl.BlockSpec((slots, hidden), lambda i: (0, 0))
    return pl.pallas_call(
        functools.partial(finish_kernel, shards),
        grid=(steps,),
        out_shape=[
            jax.ShapeDtypeStruct((tokens, hidden), jnp.bfloat16),
            jax.ShapeDtypeStruct((shards, tokens), jnp.float32),
        ],
        in_specs=[row, row, whole, whole, rows],
        out_specs=[rows, pl.BlockSpec((shards, step), lambda i: (0, i))],
        compiler_params=pltpu.CompilerParams(vmem_limit_bytes=24 * 1024 * 1024),
        cost_estimate=pl.CostEstimate(
            flops=4 * tokens * hidden * slots, bytes_accessed=8 * tokens * hidden, transcendentals=0
        ),
    )(local, gate_prob.reshape(1, tokens), back, across, hidden_in)


def body(grad_out, hidden_in, gate_prob, expert_ids, w_down):
    tokens, width = grad_out.shape
    groups = lax.axis_size("expert")
    shards = lax.axis_size("tensor")
    chips = shards // CORES
    experts = w_down.shape[0] * groups
    capacity = 2 * tokens // experts
    share = capacity // CORES
    slots = experts * capacity
    weight = w_down[0]
    hidden = weight.shape[0]
    bf16, f32 = jnp.bfloat16, jnp.float32

    position = lax.axis_index("tensor").astype(jnp.int32)
    chip, core = position // CORES, position % CORES
    core_pairs = [(p, p ^ 1) for p in range(shards)]

    def line(array, pairs, flip=0):
        return lax.ppermute(
            array, "tensor", [(a * CORES + c, b * CORES + (c ^ flip)) for a, b in pairs for c in range(CORES)]
        )

    def swap(array):
        return lax.ppermute(array, "tensor", core_pairs)

    with jax.named_scope("route"):
        send, target = pl.pallas_call(
            functools.partial(route_kernel, capacity),
            out_shape=[jax.ShapeDtypeStruct((slots, width), bf16), jax.ShapeDtypeStruct((1, tokens), jnp.int32)],
        )(expert_ids.reshape(1, tokens), grad_out)

    with jax.named_scope("dispatch"):
        got = lax.all_to_all(send, "expert", split_axis=0, concat_axis=0, tiled=True)
        got = got.reshape(groups, CORES, share, width)

    with jax.named_scope("gather"):
        weights = [weight, swap(weight)]
        def part(c):
            return lax.dynamic_index_in_dim(got, c, axis=1, keepdims=False).reshape(groups * share, width)

        def gather(x, flip):
            right = line(x, [(0, 1), (1, 2), (2, 3)], flip)
            left = line(x, [(1, 0), (2, 1), (3, 2)], flip)
            right2 = line(right, [(1, 2), (2, 3)])
            left2 = line(left, [(2, 1), (1, 0)])
            last = [line(right2, [(2, 3)]), line(left2, [(1, 0)])]
            return [swap(x) if flip else x, right, left, right2, left2], last

        (near, last), (crossed, crossed_last) = gather(part(core), 0), gather(part(1 - core), 1)

    with jax.named_scope("products"):
        where = jnp.stack([chip, core])
        total = multiply_near(where, near + crossed, weights)
        filled = multiply_last(where, chips, total, last + crossed_last, weights)

    with jax.named_scope("return"):
        back = lax.all_to_all(filled, "expert", split_axis=0, concat_axis=0, tiled=True)

    with jax.named_scope("finish"):
        share_of = target % capacity // share
        local = jnp.where(share_of == core, 0, slots // CORES) + target // capacity * share + target % share
        across = swap(back[:, hidden:])
        grad_hidden, parts = finish(local, gate_prob, back, across, hidden_in, shards)
        gate = jnp.sum(lax.all_to_all(parts, "tensor", split_axis=0, concat_axis=0, tiled=True), axis=0)
    return grad_hidden, gate


def solution(mesh):
    return jax.shard_map(
        body,
        mesh=mesh,
        in_specs=(
            P("expert", "tensor"),
            P("expert", "tensor"),
            P("expert"),
            P("expert", None),
            P("expert", "tensor", None),
        ),
        out_specs=(P("expert", "tensor"), P("expert")),
        check_vma=False,
    )
```
